256 devices in a mesh: dp: 32 (over y_hi, z, core), tensor: 8 (over x, y_lo).
Axes of the slice: x: 4, y: 4 (y_hi: 2, y_lo: 2; y = y_hi * 2 + y_lo), z: 8, core: 2. Of those that a mesh axis runs over, the one named last changes fastest.
Arguments:
- activations: bfloat16 [16384, 8192], P('dp', 'tensor'), may hold values from -6 to 6
- cotangent: bfloat16 [16384, 1024], P('dp', 'tensor'), may hold values from -6 to 6
- weight: bfloat16 [8192, 1024], P(None, 'tensor'), may hold values from -0.0625 to 0.0625
- momentum: float32 [32, 8192, 1024], P('dp', None, 'tensor'), may hold values from -24 to 24
- band_anchor: int32 [128, 16, 2], P(None, 'tensor'), may hold values from 0 to 8
Outputs:
- input_grad: bfloat16 [16384, 8192], P('dp', 'tensor')
- new_momentum: float32 [32, 8192, 1024], P('dp', None, 'tensor')
- weight_step: bfloat16 [8192, 1024], P(None, 'tensor')
The draws below stay inside these ranges and needn't reach their ends.
Inputs may be any that keep to these rules, and one draw needn't show every extreme that they name: `band_anchor`: for every group the band of 8 x 8 frequencies from this anchor lies inside the group; all workers share the anchors.
All inputs are finite; a program needn't handle non-finite values.
Results may differ from the reference program's by a relative error of at most 0.001.
Values may be sent and summed in bfloat16 or wider, within the bound.
No kernel may reach another device: no remote copies, remote signals or barrier semaphores. Data moves between devices by JAX's collectives and lax.ppermute only.
A program may use at most 128 MiB of HBM per device.

```python
import jax
import jax.numpy as jnp
from jax import lax

D = 8192
KV = 1024
TOK_DEV = 512
GROUP = 64
BAND = 8
TOKENS = 16384
WORKERS = 32


def touch_ends(array, stream_key, least, largest):
    index_at = [jax.random.randint(jax.random.fold_in(stream_key, axis), (), 0, length) for axis, length in enumerate(array.shape)]
    longest = array.shape.index(max(array.shape))
    beside = index_at[:longest] + [(index_at[longest] + 1) % array.shape[longest]] + index_at[longest + 1:]
    return array.at[tuple(index_at)].set(least).at[tuple(beside)].set(largest)


def shard_levels(key, shape, pieces, low, largest):
    def one(position, blocks):
        steps = jax.random.uniform(jax.random.fold_in(jax.random.fold_in(key, 6), position), (blocks,), jnp.float32, low / len(pieces), largest / len(pieces))
        return jnp.repeat(jnp.exp(steps), shape[position] // blocks).reshape((-1,) + (1,) * (len(shape) - position - 1))

    gain = one(*pieces[0])
    for cut in pieces[1:]:
        gain = gain * one(*cut)
    return gain


def normal_values(stream_key, extent, scale, bound, split=(), kind=jnp.bfloat16):
    values = scale * jax.random.normal(stream_key, extent, jnp.float32)
    if split:
        values = values * shard_levels(stream_key, extent, split, -0.22, 0.18)
    return jnp.clip(values, -bound, bound).astype(kind)


def setup_inputs(seed: int = 0) -> dict:
    streams_of = jax.random.split(jax.random.key(seed), 6)
    return {
        "activations": normal_values(streams_of[0], (TOKENS, D), 1.0, 6.0, ((0, 32), (1, 8))),
        "cotangent": normal_values(streams_of[1], (TOKENS, KV), 1.0, 6.0, ((0, 32), (1, 8))),
        "weight": normal_values(streams_of[2], (D, KV), D ** -0.5, 0.0625, ((1, 8),)),
        "momentum": normal_values(streams_of[3], (WORKERS, D, KV), 4.0, 24.0, ((0, 32), (2, 8)), jnp.float32),
        "band_anchor": touch_ends(jax.random.randint(streams_of[4], (D // GROUP, KV // GROUP, 2), 0, GROUP // 8 + 1), jax.random.fold_in(streams_of[4], 1), 0, (GROUP // 8 + 1) - 1).astype(jnp.int32),
    }


PRECISE = lax.Precision.HIGHEST
MOMENTUM_DECAY = 0.9

def cosine_basis(length):
    freq_index = jnp.arange(length, dtype=jnp.float32)[:, None]
    cell_index = jnp.arange(length, dtype=jnp.float32)[None, :]
    norm_scale = jnp.where(freq_index == 0, jnp.sqrt(1.0 / length), jnp.sqrt(2.0 / length))
    return (norm_scale * jnp.cos(jnp.pi * (2.0 * cell_index + 1.0) * freq_index / (2.0 * length))).astype(jnp.float32)

def rebuild(low_band, row_basis, col_basis):
    partial_value = jnp.einsum('klij,kljb->klib', low_band, col_basis, precision=PRECISE)
    blocks = jnp.einsum('klia,klib->kalb', row_basis, partial_value, precision=PRECISE)
    return blocks.reshape(D, KV)

def reference(activations, cotangent, weight, momentum, band_anchor):
    row_groups = D // GROUP
    col_groups = KV // GROUP
    cosine_table = cosine_basis(GROUP)
    offsets = jnp.arange(BAND, dtype=jnp.int32)
    row_pick = (band_anchor[:, :, 0:1] + offsets).astype(jnp.int32)
    col_pick = (band_anchor[:, :, 1:2] + offsets).astype(jnp.int32)
    row_basis = jnp.take(cosine_table, row_pick, axis=0)
    col_basis = jnp.take(cosine_table, col_pick, axis=0)
    input_grad = jnp.dot(cotangent, weight.T, preferred_element_type=jnp.float32).astype(jnp.bfloat16)

    def one_worker(inputs):
        x_rows, cot_rows, carried = inputs
        weight_grad = jnp.dot(x_rows.T, cot_rows, preferred_element_type=jnp.float32)
        moment = MOMENTUM_DECAY * carried + weight_grad
        blocks = moment.reshape(row_groups, GROUP, col_groups, GROUP)
        partial_value = jnp.einsum('klia,kalb->klib', row_basis, blocks, precision=PRECISE)
        low_band = jnp.einsum('klib,kljb->klij', partial_value, col_basis, precision=PRECISE)
        return (moment - rebuild(low_band, row_basis, col_basis), low_band)
    x_split = activations.reshape(WORKERS, TOK_DEV, D)
    cot_split = cotangent.reshape(WORKERS, TOK_DEV, KV)
    new_momentum, all_bands = lax.map(one_worker, (x_split, cot_split, momentum))
    band_total = lax.optimization_barrier(jnp.sum(all_bands, axis=0))
    weight_step = rebuild(band_total, row_basis, col_basis).astype(jnp.bfloat16)
    return (input_grad, new_momentum, weight_step)
```

```python
import functools

import jax
import jax.numpy as jnp
import numpy as np
from jax import lax
from jax.experimental import pallas as pl
from jax.experimental.pallas import tpu as pltpu
from jax.sharding import Mesh
from jax.sharding import PartitionSpec as P

GROUP = 64
BAND = 8
FREQ = 16
DECAY = 0.9
LIMIT = 20.0

F32, BF16, F16 = jnp.float32, jnp.bfloat16, jnp.float16
TENSOR = ("x", "yl")
NT = (((1,), (1,)), ((), ()))


def split_const(a):
    a = np.asarray(a, np.float32)
    hi = a.astype(jnp.bfloat16)
    lo = (a - hi.astype(np.float32)).astype(jnp.bfloat16)
    return hi, lo


def tables():
    f = np.arange(FREQ)[:, None]
    a = np.arange(GROUP)[None, :]
    scale = np.where(f == 0, np.sqrt(1 / GROUP), np.sqrt(2 / GROUP))
    c16 = scale * np.cos(np.pi * (2 * a + 1) * f / (2 * GROUP))
    rows = np.kron(np.eye(4), c16)
    cols = np.tile(np.kron(np.eye(2), c16.T), (1, 4))
    rh, rl = split_const(rows)
    th, tl = split_const(rows.T)
    ch, cl = split_const(cols)
    uh, ul = split_const(cols.T)
    place = [
        np.kron(np.kron(np.eye(8), pick), np.ones((1, FREQ)))
        for pick in ([[1], [0]], [[0], [1]])
    ]
    return np.concatenate(
        [
            rh,
            rl,
            np.concatenate([th, tl, th, np.zeros_like(th)], axis=1),
            np.concatenate([ch, cl], axis=1),
            np.concatenate([uh, ul], axis=1),
            np.concatenate(place, axis=1).astype(rh.dtype),
        ],
        axis=0,
    )


ROWS = slice(0, 128)
ROWS_T = slice(128, 384)
COLS = slice(384, 512)
COLS_T = slice(512, 640)
PLACE = slice(640, 656)


def split(a):
    hi = a.astype(BF16)
    return hi, (a - hi.astype(F32)).astype(BF16)


def mm(a, b):
    return jnp.dot(a, b, preferred_element_type=F32)


def times_table(a, table):
    hi, lo = split(a)
    both = mm(hi, table)
    return both[:, :128] + (both[:, 128:] + mm(lo, table[:, :128]))


def lane_block(shape, kk):
    lane = lax.broadcasted_iota(jnp.int32, shape, len(shape) - 1)
    return lane // 32 == kk


def pick_lanes(parts):
    out = parts[0]
    for kk in range(1, 4):
        out = jnp.where(lane_block(out.shape, kk), parts[kk], out)
    return out


def moment_band_kernel(m_ref, table_ref, o_ref):
    z = []
    for q in range(4):
        m = jnp.concatenate(split(m_ref[q * 256 : (q + 1) * 256, :]), axis=1)
        v = mm(table_ref[ROWS, :], m)
        z.append(v[:64, :128] + (v[:64, 128:] + v[64:, :128]))
    y = times_table(jnp.concatenate(z, axis=0), table_ref[COLS, :])
    for q in range(4):
        o_ref[0, q * 16 : (q + 1) * 16, :] = pick_lanes(
            [y[q * 64 + kk * 16 : q * 64 + (kk + 1) * 16] for kk in range(4)]
        )


def grad_band_kernel(a_ref, cot_ref, table_ref, o_ref):
    high, low = [], []
    for q in range(4):
        v = lax.dot_general(
            table_ref[ROWS, :], a_ref[:, q * 256 : (q + 1) * 256], NT, preferred_element_type=F32
        )
        h, l = split(v[:64] + v[64:])
        high.append(h)
        low.append(l)
    high, low = jnp.concatenate(high, axis=0), jnp.concatenate(low, axis=0)
    for j in range(0, 8, 2):
        halves = []
        for i in (j, j + 1):
            both = mm(cot_ref[i, :512, :], table_ref[COLS, :])
            halves.append(split(both[:, :128] + both[:, 128:]))
        rh = jnp.concatenate([halves[0][0], halves[1][0]], axis=1)
        rl = jnp.concatenate([halves[0][1], halves[1][1]], axis=1)
        x = mm(high, rh) + (mm(high, rl) + mm(low, rh))
        for i in (0, 1):
            for q in range(4):
                o_ref[j + i, q * 16 : (q + 1) * 16, :] = pick_lanes(
                    [
                        x[q * 64 + kk * 16 : q * 64 + (kk + 1) * 16, i * 128 : (i + 1) * 128]
                        for kk in range(4)
                    ]
                )


def band_mask(anchor, place):
    at = mm(anchor, place)
    r, c = at[:, None, :128], at[:, None, 128:]
    shape = (32, FREQ, 128)
    f = lax.broadcasted_iota(jnp.int32, shape, 1).astype(F32)
    g = (lax.broadcasted_iota(jnp.int32, shape, 2) % FREQ).astype(F32)
    inside = (f >= r) & (f < r + BAND) & (g >= c) & (g < c + BAND)
    return jnp.where(inside, 1.0, 0.0).astype(F32)


def pack_kernel(xm_ref, xg_ref, a_ref, table_ref, low_ref, pack_ref):
    mask = band_mask(a_ref[...], table_ref[PLACE, :]).reshape(8, 64, 128)
    low = mask * (xg_ref[...] + DECAY * xm_ref[...])
    low_ref[...] = low
    rows = low.reshape(8, 4, 2, 8, 128)
    rows = (rows[:, :, 0] + rows[:, :, 1]).reshape(2, 128, 128)
    a, b = rows[0], rows[1]
    lane = lax.broadcasted_iota(jnp.int32, a.shape, 1)
    pack_ref[...] = jnp.where(lane % 16 < 8, a + pltpu.roll(a, 120, 1), b + pltpu.roll(b, 8, 1))


def unpack(p, mask):
    lane = lax.broadcasted_iota(jnp.int32, p.shape, 1)
    low = lane % 16 < 8
    a = jnp.where(low, p, pltpu.roll(p, 8, 1))
    b = jnp.where(low, pltpu.roll(p, 120, 1), p)
    r = jnp.concatenate([a, b], axis=0).reshape(8, 4, 1, 8, 128)
    r = jnp.broadcast_to(r, (8, 4, 2, 8, 128)).reshape(8, 64, 128)
    return r * mask


def rebuild_chunk(low, table_ref):
    spread = []
    for q in range(4):
        part = low[q * 16 : (q + 1) * 16]
        spread += [jnp.where(lane_block(part.shape, kk), part, 0.0) for kk in range(4)]
    v = times_table(jnp.concatenate(spread, axis=0), table_ref[COLS_T, :])
    out = []
    for q in (0, 2):
        pair = jnp.concatenate([v[q * 64 : (q + 1) * 64], v[(q + 1) * 64 : (q + 2) * 64]], axis=1)
        hi, lo = split(pair)
        both = mm(table_ref[ROWS_T, :192], jnp.concatenate([hi, hi, lo], axis=0))
        out += [both[:, :128], both[:, 128:]]
    return out


def rest_kernel(low_ref, m_ref, table_ref, o_ref):
    for q, v in enumerate(rebuild_chunk(low_ref[0], table_ref)):
        rows = slice(q * 256, (q + 1) * 256)
        o_ref[0, rows, :] = DECAY * m_ref[rows, :] - v


def step_kernel(pack_ref, a_ref, table_ref, o_ref, low_ref):
    @pl.when(pl.program_id(0) == 0)
    def _():
        mask = band_mask(a_ref[...], table_ref[PLACE, :]).reshape(8, 64, 128)
        low_ref[...] = unpack(pack_ref[...], mask)

    for q, v in enumerate(rebuild_chunk(low_ref[pl.program_id(0)], table_ref)):
        o_ref[q * 256 : (q + 1) * 256, :] = v.astype(BF16)


def input_kernel(cot_ref, w_ref, o_ref):
    lhs = jnp.concatenate([cot_ref[j, :512, :] for j in range(8)], axis=1)
    count, _, part, _ = w_ref.shape
    step = max(1, 256 // part)
    size = step * part
    for i in range(0, count, step):
        rhs = jnp.concatenate(
            [w_ref[i : i + step, j].reshape(size, 128) for j in range(8)], axis=1
        )
        v = lax.dot_general(lhs, rhs, NT, preferred_element_type=F32)
        o_ref[:, i * part : i * part + size] = v.astype(BF16)


def whole(a):
    return pl.BlockSpec(a.shape, lambda i: (0,) * a.ndim)


def params(mib=16):
    return pltpu.CompilerParams(vmem_limit_bytes=mib * 2**20)


def cost(mflops, kib):
    return pl.CostEstimate(
        flops=mflops * 10**6, bytes_accessed=kib * 2**10, transcendentals=0
    )


def exchange_sum(v, axes, sizes, moves):
    n = int(np.prod([sizes[a] for a in axes]))
    moves = [m for m in moves if m < n]
    got = [lax.ppermute(v, axes, [(i, i ^ m) for i in range(n)]) for m in moves]
    if len(got) == 3:
        return (v + got[0]) + (got[1] + got[2])
    return v + got[0] if got else v


def body(sizes, activations, cotangent, weight, momentum, band_anchor):
    table = jnp.asarray(tables())
    nz, nc = sizes["z"], sizes["c"]
    moment0 = momentum[0]
    anchor = band_anchor.reshape(32, 16).astype(BF16)

    part = 1024 // (nz * nc)
    with jax.named_scope("gather_cotangent"):
        at = (lax.axis_index("z") * nc + lax.axis_index("c")) * part
        mine = lax.dynamic_slice(weight.reshape(8, 1024, 128), (0, at, 0), (8, part, 128))
        sent = jnp.concatenate([jnp.broadcast_to(cotangent, (8, 512, 128)), mine], axis=1)
        got = lax.all_to_all(sent, TENSOR, 0, 0)

    with jax.named_scope("share_weight"):
        rows_all = lax.all_gather(got[:, 512:], ("z", "c"))

    with jax.named_scope("moment_band"):
        moment_band = pl.pallas_call(
            moment_band_kernel,
            grid=(8,),
            in_specs=[pl.BlockSpec((1024, 128), lambda i: (i, 0)), whole(table)],
            out_specs=pl.BlockSpec((1, 64, 128), lambda i: (i, 0, 0)),
            out_shape=jax.ShapeDtypeStruct((8, 64, 128), F32),
            compiler_params=params(),
            cost_estimate=cost(2000, 4096),
        )(moment0, table)

    own_scale = jnp.maximum(jnp.max(jnp.abs(cotangent), axis=0).astype(F32), 1e-30) / LIMIT

    with jax.named_scope("grad_band"):
        grad_band = pl.pallas_call(
            grad_band_kernel,
            out_shape=jax.ShapeDtypeStruct((8, 64, 128), F32),
            compiler_params=params(),
            cost_estimate=cost(2000, 2048),
        )(activations, got, table)
        got, grad_band = lax.optimization_barrier((got, grad_band))
        grad_band = lax.all_to_all(grad_band, TENSOR, 0, 0)

    with jax.named_scope("weight_grad"):
        cot8 = got[:, :512]
        top = jnp.max(jnp.abs(cot8), axis=1).astype(F32)
        top = jnp.maximum(top, 1e-30)
        grad = jnp.einsum("tf,jtc->fjc", activations, cot8, preferred_element_type=F32)
        grad = jnp.moveaxis((grad * (LIMIT / top)).astype(F16), 1, 0)
        grad, grad_band = lax.optimization_barrier((grad, grad_band))
        grad = lax.all_to_all(grad, TENSOR, 0, 0)

    with jax.named_scope("pack"):
        low, packed = pl.pallas_call(
            pack_kernel,
            out_shape=[
                jax.ShapeDtypeStruct((8, 64, 128), F32),
                jax.ShapeDtypeStruct((128, 128), F32),
            ],
            compiler_params=params(),
            cost_estimate=cost(100, 1024),
        )(moment_band, grad_band, anchor, table)

    with jax.named_scope("band_total"):
        packed = exchange_sum(packed, ("z", "c"), sizes, (2, 4, 6))
        packed = exchange_sum(packed, ("z", "c"), sizes, (1, 8, 9))
        packed = exchange_sum(packed, ("yh",), sizes, (1,))

    with jax.named_scope("rest"):
        rest = pl.pallas_call(
            rest_kernel,
            grid=(8,),
            in_specs=[
                pl.BlockSpec((1, 64, 128), lambda i: (i, 0, 0)),
                pl.BlockSpec((1024, 128), lambda i: (i, 0)),
                whole(table),
            ],
            out_specs=pl.BlockSpec((1, 1024, 128), lambda i: (i, 0, 0)),
            out_shape=jax.ShapeDtypeStruct((8, 1024, 128), F32),
            compiler_params=params(),
            cost_estimate=cost(3000, 8192),
        )(low, moment0, table)

    with jax.named_scope("input_grad"):
        input_grad = pl.pallas_call(
            input_kernel,
            out_shape=jax.ShapeDtypeStruct((512, 1024), BF16),
            compiler_params=params(),
            cost_estimate=cost(1000, 4096),
        )(got, rows_all)

    with jax.named_scope("weight_step"):
        weight_step = pl.pallas_call(
            step_kernel,
            grid=(8,),
            in_specs=[whole(a) for a in (packed, anchor, table)],
            out_specs=pl.BlockSpec((1024, 128), lambda i: (i, 0)),
            out_shape=jax.ShapeDtypeStruct((8192, 128), BF16),
            scratch_shapes=[pltpu.VMEM((8, 64, 128), F32)],
            compiler_params=params(),
            cost_estimate=cost(3000, 2048),
        )(packed, anchor, table)

    with jax.named_scope("new_momentum"):
        new_momentum = rest + grad.astype(F32) * own_scale

    return (input_grad, new_momentum.reshape(1, 8192, 128), weight_step)


def solution(mesh):
    shape = (2, 8, 2, 4, 2)
    if mesh.devices.size == 16:
        shape = (1, 1, 2, 4, 2)
    names = ("yh", "z", "c", "x", "yl")
    fine = Mesh(mesh.devices.reshape(shape), names)
    dp = ("yh", "z", "c")
    return jax.shard_map(
        functools.partial(body, dict(zip(names, shape))),
        mesh=fine,
        in_specs=(
            P(dp, TENSOR),
            P(dp, TENSOR),
            P(None, TENSOR),
            P(dp, None, TENSOR),
            P(None, TENSOR, None),
        ),
        out_specs=(P(dp, TENSOR), P(dp, None, TENSOR), P(None, TENSOR)),
        check_vma=False,
    )
```

```python
import functools

import jax
import jax.numpy as jnp
import numpy as np
from jax import lax
from jax.experimental import pallas as pl
from jax.experimental.pallas import tpu as pltpu
from jax.sharding import Mesh
from jax.sharding import PartitionSpec as P

GROUP = 64
BAND = 8
FREQ = 16
DECAY = 0.9
LIMIT = 20.0

F32, BF16, F16 = jnp.float32, jnp.bfloat16, jnp.float16
TENSOR = ("x", "yl")
NT = (((1,), (1,)), ((), ()))


def split_const(a):
    a = np.asarray(a, np.float32)
    hi = a.astype(jnp.bfloat16)
    lo = (a - hi.astype(np.float32)).astype(jnp.bfloat16)
    return hi, lo


def tables():
    f = np.arange(FREQ)[:, None]
    a = np.arange(GROUP)[None, :]
    scale = np.where(f == 0, np.sqrt(1 / GROUP), np.sqrt(2 / GROUP))
    c16 = scale * np.cos(np.pi * (2 * a + 1) * f / (2 * GROUP))
    rows = np.kron(np.eye(4), c16)
    cols = np.tile(np.kron(np.eye(2), c16.T), (1, 4))
    rh, rl = split_const(rows)
    th, tl = split_const(rows.T)
    ch, cl = split_const(cols)
    uh, ul = split_const(cols.T)
    return np.concatenate(
        [
            rh,
            rl,
            np.concatenate([th, tl, th, np.zeros_like(th)], axis=1),
            np.concatenate([ch, cl], axis=1),
            np.concatenate([uh, ul], axis=1),
        ],
        axis=0,
    )


ROWS = slice(0, 128)
ROWS_T = slice(128, 384)
COLS = slice(384, 512)
COLS_T = slice(512, 640)


def split(a):
    hi = a.astype(BF16)
    return hi, (a - hi.astype(F32)).astype(BF16)


def mm(a, b):
    return jnp.dot(a, b, preferred_element_type=F32)


def times_table(a, table):
    hi, lo = split(a)
    both = mm(hi, table)
    return both[:, :128] + (both[:, 128:] + mm(lo, table[:, :128]))


def lane_block(shape, kk):
    lane = lax.broadcasted_iota(jnp.int32, shape, len(shape) - 1)
    return lane // 32 == kk


def pick_lanes(parts):
    out = parts[0]
    for kk in range(1, 4):
        out = jnp.where(lane_block(out.shape, kk), parts[kk], out)
    return out


def anchor_lanes(anchor_ref):
    row = lax.broadcasted_iota(jnp.int32, (32, 128), 0)
    group = lax.broadcasted_iota(jnp.int32, (32, 128), 1)
    own = group // 4 == row
    group = lax.broadcasted_iota(jnp.int32, (128, 128), 0)
    lane = lax.broadcasted_iota(jnp.int32, (128, 128), 1)
    out = []
    for which in range(2):
        v = jnp.zeros((32, 128), F32)
        for l in range(2):
            at = jnp.where(own, anchor_ref[l, which : which + 1, :].astype(F32), 0.0)
            to = (group % 4 == lane // 32) & (lane // FREQ % 2 == l)
            v += mm(at.astype(BF16), jnp.where(to, 1.0, 0.0).astype(BF16))
        out.append(v)
    return out


def band_mask(r, c):
    f = lax.broadcasted_iota(jnp.int32, (FREQ, 128), 0).astype(F32)
    g = (lax.broadcasted_iota(jnp.int32, (FREQ, 128), 1) % FREQ).astype(F32)
    out = []
    for q in range(4):
        rq, cq = r[q : q + 1, :], c[q : q + 1, :]
        inside = (f >= rq) & (f < rq + BAND) & (g >= cq) & (g < cq + BAND)
        out.append(jnp.where(inside, 1.0, 0.0))
    return jnp.concatenate(out, axis=0)


def row_bands(m, table_ref, z_ref, t):
    for q in range(4):
        both = jnp.concatenate(split(m[q * 256 : (q + 1) * 256, :]), axis=1)
        v = mm(table_ref[ROWS, :], both)
        z_ref[t, q * 64 : (q + 1) * 64, :] = v[:64, :128] + (v[:64, 128:] + v[64:, :128])


def column_bands(table_ref, z_ref, low_ref, r, c):
    for t in range(8):
        y = times_table(z_ref[t], table_ref[COLS, :])
        for q in range(4):
            low_ref[t, q * 16 : (q + 1) * 16, :] = pick_lanes(
                [y[q * 64 + kk * 16 : q * 64 + (kk + 1) * 16] for kk in range(4)]
            )
        low_ref[t] = low_ref[t] * band_mask(r[4 * t : 4 * t + 4], c[4 * t : 4 * t + 4])


def moment_band_kernel(m_hbm, a_hbm, anchor_ref, table_ref, low_ref, act_ref, *scratch):
    m_ref, a_ref, z_ref, sems = scratch
    get_m = [
        pltpu.make_async_copy(m_hbm.at[pl.ds(t * 1024, 1024)], m_ref.at[t], sems.at[t])
        for t in range(8)
    ]
    get_a = pltpu.make_async_copy(a_hbm, a_ref, sems.at[8])
    get_a.start()
    for copy in get_m:
        copy.start()
    r, c = anchor_lanes(anchor_ref)
    get_a.wait()
    for q in range(4):
        v = lax.dot_general(
            table_ref[ROWS, :], a_ref[:, q * 256 : (q + 1) * 256], NT, preferred_element_type=F32
        )
        rows = slice(q * 64, (q + 1) * 64)
        act_ref[0, rows, :], act_ref[1, rows, :] = split(v[:64] + v[64:])
    for t in range(8):
        get_m[t].wait()
        row_bands(m_ref.at[t], table_ref, z_ref, t)
    column_bands(table_ref, z_ref, low_ref, r, c)
    low_ref[...] = DECAY * low_ref[...]


def send_kernel(cot_hbm, w_hbm, o_hbm, cot_ref, w_ref, sems):
    part = w_ref.shape[1]
    at = pl.multiple_of(share_index(part) * part, part)
    get_w = pltpu.make_async_copy(w_hbm.at[:, pl.ds(at, part)], w_ref, sems.at[0])
    get_cot = pltpu.make_async_copy(cot_hbm, cot_ref, sems.at[1])
    put_w = pltpu.make_async_copy(w_ref, o_hbm.at[:, pl.ds(512, part)], sems.at[2])
    put_cot = [
        pltpu.make_async_copy(cot_ref, o_hbm.at[j, pl.ds(0, 512)], sems.at[3 + j])
        for j in range(8)
    ]
    get_cot.start()
    get_w.start()
    get_cot.wait()
    for copy in put_cot:
        copy.start()
    get_w.wait()
    put_w.start()
    for copy in put_cot:
        copy.wait()
    put_w.wait()


def share_index(part, core=0, z=0):
    pairs = 1024 // (part * lax.axis_size("c"))
    mine = jnp.bitwise_xor(lax.axis_index("c"), core) * pairs
    if pairs > 1:
        mine = mine + jnp.bitwise_xor(lax.rem(lax.axis_index("z"), 2), z)
    return mine


def grad_band_kernel(act_hbm, cot_ref, table_hbm, o_hbm, *scratch):
    act_ref, table_ref, out, sems = scratch
    get_table = pltpu.make_async_copy(table_hbm.at[COLS], table_ref, sems.at[0])
    get_act = pltpu.make_async_copy(act_hbm, act_ref, sems.at[1])
    put = []
    for copy in (get_table, get_act):
        copy.start()
    get_table.wait()
    get_act.wait()
    high, low = act_ref[0], act_ref[1]
    for j in range(0, 8, 2):
        halves = []
        for i in range(2):
            both = mm(cot_ref[j + i, :512, :], table_ref[...])
            halves.append(split(both[:, :128] + both[:, 128:]))
        rh = jnp.concatenate([halves[0][0], halves[1][0]], axis=1)
        rl = jnp.concatenate([halves[0][1], halves[1][1]], axis=1)
        x = mm(high, rh) + (mm(high, rl) + mm(low, rh))
        for i in range(2):
            for q in range(4):
                out[j + i, q * 16 : (q + 1) * 16, :] = pick_lanes(
                    [
                        x[q * 64 + kk * 16 : q * 64 + (kk + 1) * 16, i * 128 : (i + 1) * 128]
                        for kk in range(4)
                    ]
                )
        two = pl.ds(j, 2)
        put.append(pltpu.make_async_copy(out.at[two], o_hbm.at[two], sems.at[5 + j // 2]))
        put[-1].start()
    for copy in put:
        copy.wait()


def pack_kernel(moment_hbm, grad_ref, anchor_ref, low_ref, keep_ref, give_ref, *scratch):
    moment_ref, pack_ref, sem = scratch
    get = pltpu.make_async_copy(moment_hbm, moment_ref, sem)
    get.start()
    r, c = anchor_lanes(anchor_ref)
    get.wait()
    for t in range(8):
        mask = band_mask(r[4 * t : 4 * t + 4], c[4 * t : 4 * t + 4])
        low_ref[t] = mask * grad_ref[t] + moment_ref[t]
    rows = low_ref[...].reshape(8, 4, 2, 8, 128)
    rows = (rows[:, :, 0] + rows[:, :, 1]).reshape(2, 128, 128)
    a, b = rows[0], rows[1]
    lane = lax.broadcasted_iota(jnp.int32, a.shape, 1)
    pack_ref[...] = jnp.where(lane % 16 < 8, a + pltpu.roll(a, 120, 1), b + pltpu.roll(b, 8, 1))
    core = lax.axis_index("c")
    keep_ref[...] = pack_ref[core_rows(core), :]
    give_ref[...] = pack_ref[core_rows(1 - core), :]


def core_rows(core):
    return pl.ds(pl.multiple_of(core * 64, 64), 64)


def unpack(p):
    low = lax.broadcasted_iota(jnp.int32, p.shape, 1) % 16 < 8
    a = jnp.where(low, p, pltpu.roll(p, 8, 1))
    b = jnp.where(low, pltpu.roll(p, 120, 1), p)
    r = jnp.concatenate([a, b], axis=0).reshape(8, 4, 1, 8, 128)
    return jnp.broadcast_to(r, (8, 4, 2, 8, 128)).reshape(8, 64, 128)


def rebuild(low_ref, table_ref, v_ref, emit):
    for t in range(8):
        spread = []
        for q in range(4):
            part = low_ref[t, q * 16 : (q + 1) * 16, :]
            spread += [jnp.where(lane_block(part.shape, kk), part, 0.0) for kk in range(4)]
        v = times_table(jnp.concatenate(spread, axis=0), table_ref[COLS_T, :])
        for n in range(2):
            rows = [v[(2 * n + i) * 64 : (2 * n + i + 1) * 64] for i in range(2)]
            hi, lo = split(jnp.concatenate(rows, axis=1))
            v_ref[t, n] = jnp.concatenate([hi, hi, lo], axis=0)
    for t in range(8):
        for n in range(2):
            both = mm(table_ref[ROWS_T, :192], v_ref[t, n])
            emit(t, 2 * n, both[:, :128])
            emit(t, 2 * n + 1, both[:, 128:])


def rest_kernel(low_ref, m_hbm, table_hbm, o_hbm, table_ref, m_ref, v_ref, sems):
    get_table = pltpu.make_async_copy(table_hbm, table_ref, sems.at[1])
    get_m = [
        pltpu.make_async_copy(m_hbm.at[pl.ds(t * 1024, 1024)], m_ref.at[t], sems.at[2 + t])
        for t in range(8)
    ]
    put = [pltpu.make_async_copy(m_ref.at[t], o_hbm.at[t], sems.at[10 + t]) for t in range(8)]
    for copy in [get_table] + get_m:
        copy.start()
    get_table.wait()

    def emit(t, q, v):
        if q == 0:
            get_m[t].wait()
        rows = slice(q * 256, (q + 1) * 256)
        m_ref[t, rows, :] = DECAY * m_ref[t, rows, :] - v
        if q == 3:
            put[t].start()

    rebuild(low_ref, table_ref, v_ref, emit)
    for copy in put:
        copy.wait()


def step_kernel(mine_ref, other_ref, anchor_ref, table_hbm, o_hbm, *scratch):
    low_ref, pack_ref, table_ref, v_ref, o_ref, sems = scratch
    get_table = pltpu.make_async_copy(table_hbm, table_ref, sems.at[8])
    put = [
        pltpu.make_async_copy(o_ref.at[t], o_hbm.at[pl.ds(t * 1024, 1024)], sems.at[t])
        for t in range(8)
    ]
    get_table.start()
    core = lax.axis_index("c")
    pack_ref[core_rows(core), :] = mine_ref[...]
    pack_ref[core_rows(1 - core), :] = other_ref[...]
    r, c = anchor_lanes(anchor_ref)
    low_ref[...] = unpack(pack_ref[...])
    for t in range(8):
        low_ref[t] = low_ref[t] * band_mask(r[4 * t : 4 * t + 4], c[4 * t : 4 * t + 4])
    get_table.wait()

    def emit(t, q, v):
        o_ref[t, q * 256 : (q + 1) * 256, :] = v.astype(BF16)
        if q == 3:
            put[t].start()

    rebuild(low_ref, table_ref, v_ref, emit)
    for copy in put:
        copy.wait()


def input_kernel(cot_hbm, *refs):
    count = len(refs) - 5
    w_hbm, o_hbm = refs[:count], refs[count]
    cot_ref, w_ref, o_ref, sems = refs[count + 1 :]
    part = w_ref.shape[2]
    get_cot = [
        pltpu.make_async_copy(
            cot_hbm.at[j, pl.ds(0, 512)], cot_ref.at[:, pl.ds(j * 128, 128)], sems.at[j]
        )
        for j in range(8)
    ]
    get_w = [pltpu.make_async_copy(w_hbm[n], w_ref.at[n], sems.at[8 + n]) for n in range(count)]
    for copy in get_cot + get_w:
        copy.start()
    put = []
    for copy in get_cot:
        copy.wait()
    for n in range(count):
        get_w[n].wait()
        rhs = jnp.concatenate([w_ref[n, j] for j in range(8)], axis=1)
        v = lax.dot_general(cot_ref[...], rhs, NT, preferred_element_type=F32)
        o_ref[n] = v.astype(BF16)
        share = share_index(part, n % 2, n // 2)
        lanes = pl.ds(pl.multiple_of(share * part, part), part)
        put.append(pltpu.make_async_copy(o_ref.at[n], o_hbm.at[:, lanes], sems.at[12 + n]))
        put[-1].start()
    for copy in put:
        copy.wait()


HBM = pl.BlockSpec(memory_space=pltpu.HBM)
VMEM = pl.BlockSpec(memory_space=pltpu.VMEM)


def whole(a):
    return pl.BlockSpec(a.shape, lambda i: (0,) * a.ndim)


def params(mib=16):
    return pltpu.CompilerParams(vmem_limit_bytes=mib * 2**20)


def cost(mflops, kib):
    return pl.CostEstimate(
        flops=mflops * 10**6, bytes_accessed=kib * 2**10, transcendentals=0
    )


def exchange_sum(v, axes, sizes, move):
    n = int(np.prod([sizes[a] for a in axes]))
    if move >= n:
        return v
    return v + lax.ppermute(v, axes, [(i, i ^ move) for i in range(n)])


def body(sizes, activations, cotangent, weight, momentum, band_anchor):
    table = jnp.asarray(tables())
    nz, nc = sizes["z"], sizes["c"]
    moment0 = momentum[0]
    anchor = band_anchor.transpose(1, 2, 0)

    pairs = 2 if nz > 1 else 1
    part = 1024 // (pairs * nc)
    with jax.named_scope("gather_cotangent"):
        sent = pl.pallas_call(
            send_kernel,
            in_specs=[HBM] * 2,
            out_specs=HBM,
            out_shape=jax.ShapeDtypeStruct((8, 512 + part, 128), BF16),
            scratch_shapes=[
                pltpu.VMEM((512, 128), BF16),
                pltpu.VMEM((8, part, 128), BF16),
                pltpu.SemaphoreType.DMA((11,)),
            ],
            compiler_params=params(56),
            cost_estimate=cost(1, 2048),
        )(cotangent, weight.reshape(8, 1024, 128))
        got = lax.all_to_all(sent, TENSOR, 0, 0)

    with jax.named_scope("moment_band"):
        moment_band, act_band = pl.pallas_call(
            moment_band_kernel,
            in_specs=[HBM, HBM, VMEM, VMEM],
            out_specs=[VMEM] * 2,
            out_shape=[
                jax.ShapeDtypeStruct((8, 64, 128), F32),
                jax.ShapeDtypeStruct((2, 256, 512), BF16),
            ],
            scratch_shapes=[
                pltpu.VMEM((8, 1024, 128), F32),
                pltpu.VMEM((512, 1024), BF16),
                pltpu.VMEM((8, 256, 128), F32),
                pltpu.SemaphoreType.DMA((9,)),
            ],
            compiler_params=params(52),
            cost_estimate=cost(2000, 5120),
        )(moment0, activations, anchor, table)
        got, moment_band, act_band = lax.optimization_barrier((got, moment_band, act_band))

    own_scale = jnp.maximum(jnp.max(jnp.abs(cotangent), axis=0).astype(F32), 1e-30) / LIMIT

    swap = [(i, nc - 1 - i) for i in range(nc)]
    with jax.named_scope("weight_share"):
        share = got[:, 512:]
        shares = [share, lax.ppermute(share, "c", swap)]
        if pairs > 1:
            share = lax.ppermute(share, "z", [(k, k ^ 1) for k in range(nz)])
            shares += [share, lax.ppermute(share, "c", swap)]

    with jax.named_scope("grad_band"):
        grad_band = pl.pallas_call(
            grad_band_kernel,
            in_specs=[HBM, VMEM, HBM],
            out_specs=HBM,
            out_shape=jax.ShapeDtypeStruct((8, 64, 128), F32),
            scratch_shapes=[
                pltpu.VMEM((2, 256, 512), BF16),
                pltpu.VMEM((128, 256), BF16),
                pltpu.VMEM((8, 64, 128), F32),
                pltpu.SemaphoreType.DMA((9,)),
            ],
            compiler_params=params(40),
            cost_estimate=cost(2000, 2048),
        )(act_band, got, table)
        got, grad_band = lax.optimization_barrier((got, grad_band))
        grad_band = lax.all_to_all(grad_band, TENSOR, 0, 0)

    with jax.named_scope("weight_grad"):
        cot8 = got[:, :512]
        top = jnp.max(jnp.abs(cot8), axis=1).astype(F32)
        top = jnp.maximum(top, 1e-30)
        grad = jnp.einsum("tf,jtc->fjc", activations, cot8, preferred_element_type=F32)
        grad = jnp.moveaxis((grad * (LIMIT / top)).astype(F16), 1, 0)
        grad, grad_band, shares = lax.optimization_barrier((grad, grad_band, shares))
        grad = lax.all_to_all(grad, TENSOR, 0, 0)

    with jax.named_scope("pack"):
        low, mine, other = pl.pallas_call(
            pack_kernel,
            in_specs=[HBM, VMEM, VMEM],
            out_specs=[VMEM] * 3,
            out_shape=[jax.ShapeDtypeStruct((8, 64, 128), F32)]
            + [jax.ShapeDtypeStruct((64, 128), F32)] * 2,
            scratch_shapes=[
                pltpu.VMEM((8, 64, 128), F32),
                pltpu.VMEM((128, 128), F32),
                pltpu.SemaphoreType.DMA,
            ],
            compiler_params=params(),
            cost_estimate=cost(100, 1024),
        )(moment_band, grad_band, anchor)

    with jax.named_scope("rest"):
        rest = pl.pallas_call(
            rest_kernel,
            in_specs=[VMEM, HBM, HBM],
            out_specs=HBM,
            out_shape=jax.ShapeDtypeStruct((8, 1024, 128), F32),
            scratch_shapes=[
                pltpu.VMEM(table.shape, BF16),
                pltpu.VMEM((8, 1024, 128), F32),
                pltpu.VMEM((8, 2, 192, 256), BF16),
                pltpu.SemaphoreType.DMA((18,)),
            ],
            compiler_params=params(56),
            cost_estimate=cost(3000, 8192),
        )(low, moment0, table)

    with jax.named_scope("input_grad"):
        input_grad = pl.pallas_call(
            input_kernel,
            in_specs=[HBM] * (1 + len(shares)),
            out_specs=HBM,
            out_shape=jax.ShapeDtypeStruct((512, 1024), BF16),
            scratch_shapes=[
                pltpu.VMEM((512, 1024), BF16),
                pltpu.VMEM((len(shares), 8, part, 128), BF16),
                pltpu.VMEM((len(shares), 512, part), BF16),
                pltpu.SemaphoreType.DMA((16,)),
            ],
            compiler_params=params(16),
            cost_estimate=cost(1000, 4096),
        )(got, *shares)

    with jax.named_scope("band_total"):
        mine = mine + lax.ppermute(other, "c", swap)
        mine = exchange_sum(mine, ("z",), sizes, 1)
        mine, rest = lax.optimization_barrier((mine, rest))
        mine = exchange_sum(mine, ("z",), sizes, 3)
        mine, input_grad = lax.optimization_barrier((mine, input_grad))
        mine = exchange_sum(mine, ("z",), sizes, 7)
        mine = exchange_sum(mine, ("yh",), sizes, 1)

    with jax.named_scope("new_momentum"):
        other = lax.ppermute(mine, "c", swap)
        new_momentum = rest + grad.astype(F32) * own_scale

    with jax.named_scope("weight_step"):
        weight_step = pl.pallas_call(
            step_kernel,
            in_specs=[VMEM] * 3 + [HBM],
            out_specs=HBM,
            out_shape=jax.ShapeDtypeStruct((8192, 128), BF16),
            scratch_shapes=[
                pltpu.VMEM((8, 64, 128), F32),
                pltpu.VMEM((128, 128), F32),
                pltpu.VMEM(table.shape, BF16),
                pltpu.VMEM((8, 2, 192, 256), BF16),
                pltpu.VMEM((8, 1024, 128), BF16),
                pltpu.SemaphoreType.DMA((10,)),
            ],
            compiler_params=params(16),
            cost_estimate=cost(3000, 2048),
        )(mine, other, anchor, table)

    return (input_grad, new_momentum.reshape(1, 8192, 128), weight_step)


def solution(mesh):
    shape = (2, 8, 2, 4, 2)
    if mesh.devices.size == 16:
        shape = (1, 1, 2, 4, 2)
    names = ("yh", "z", "c", "x", "yl")
    fine = Mesh(mesh.devices.reshape(shape), names)
    dp = ("yh", "z", "c")
    return jax.shard_map(
        functools.partial(body, dict(zip(names, shape))),
        mesh=fine,
        in_specs=(
            P(dp, TENSOR),
            P(dp, TENSOR),
            P(None, TENSOR),
            P(dp, None, TENSOR),
            P(None, TENSOR, None),
        ),
        out_specs=(P(dp, TENSOR), P(dp, None, TENSOR), P(None, TENSOR)),
        check_vma=False,
    )
```

```python
import functools

import jax
import jax.numpy as jnp
import numpy as np
from jax import lax
from jax.experimental import pallas as pl
from jax.experimental.pallas import tpu as pltpu
from jax.sharding import Mesh
from jax.sharding import PartitionSpec as P

GROUP = 64
BAND = 8
FREQ = 16
DECAY = 0.9
LIMIT = 20.0

F32, BF16, F16 = jnp.float32, jnp.bfloat16, jnp.float16
TENSOR = ("x", "yl")
NT = (((1,), (1,)), ((), ()))


def split_const(a):
    a = np.asarray(a, np.float32)
    hi = a.astype(jnp.bfloat16)
    lo = (a - hi.astype(np.float32)).astype(jnp.bfloat16)
    return hi, lo


def tables():
    f = np.arange(FREQ)[:, None]
    a = np.arange(GROUP)[None, :]
    scale = np.where(f == 0, np.sqrt(1 / GROUP), np.sqrt(2 / GROUP))
    c16 = scale * np.cos(np.pi * (2 * a + 1) * f / (2 * GROUP))
    rows = np.kron(np.eye(4), c16)
    cols = np.tile(np.kron(np.eye(2), c16.T), (1, 4))
    rh, rl = split_const(rows)
    th, tl = split_const(rows.T)
    ch, cl = split_const(cols)
    uh, ul = split_const(cols.T)
    return np.concatenate(
        [
            rh,
            rl,
            np.concatenate([th, tl, th, np.zeros_like(th)], axis=1),
            np.concatenate([ch, cl], axis=1),
            np.concatenate([uh, ul], axis=1),
        ],
        axis=0,
    )


ROWS = slice(0, 128)
ROWS_T = slice(128, 384)
COLS = slice(384, 512)
COLS_T = slice(512, 640)


def split(a):
    hi = a.astype(BF16)
    return hi, (a - hi.astype(F32)).astype(BF16)


def mm(a, b):
    return jnp.dot(a, b, preferred_element_type=F32)


def times_table(a, table):
    hi, lo = split(a)
    both = mm(hi, table)
    return both[:, :128] + (both[:, 128:] + mm(lo, table[:, :128]))


def lane_block(shape, kk):
    lane = lax.broadcasted_iota(jnp.int32, shape, len(shape) - 1)
    return lane // 32 == kk


def pick_lanes(parts):
    out = parts[0]
    for kk in range(1, 4):
        out = jnp.where(lane_block(out.shape, kk), parts[kk], out)
    return out


def anchor_lanes(anchor_ref):
    row = lax.broadcasted_iota(jnp.int32, (32, 128), 0)
    group = lax.broadcasted_iota(jnp.int32, (32, 128), 1)
    own = group // 4 == row
    group = lax.broadcasted_iota(jnp.int32, (128, 128), 0)
    lane = lax.broadcasted_iota(jnp.int32, (128, 128), 1)
    out = []
    for which in range(2):
        v = jnp.zeros((32, 128), F32)
        for l in range(2):
            at = jnp.where(own, anchor_ref[l, which : which + 1, :].astype(F32), 0.0)
            to = (group % 4 == lane // 32) & (lane // FREQ % 2 == l)
            v += mm(at.astype(BF16), jnp.where(to, 1.0, 0.0).astype(BF16))
        out.append(v)
    return out


def band_mask(r, c):
    f = lax.broadcasted_iota(jnp.int32, (FREQ, 128), 0).astype(F32)
    g = (lax.broadcasted_iota(jnp.int32, (FREQ, 128), 1) % FREQ).astype(F32)
    out = []
    for q in range(4):
        rq, cq = r[q : q + 1, :], c[q : q + 1, :]
        inside = (f >= rq) & (f < rq + BAND) & (g >= cq) & (g < cq + BAND)
        out.append(jnp.where(inside, 1.0, 0.0))
    return jnp.concatenate(out, axis=0)


def row_bands(m, table_ref, z_ref, t):
    for q in range(4):
        both = jnp.concatenate(split(m[q * 256 : (q + 1) * 256, :]), axis=1)
        v = mm(table_ref[ROWS, :], both)
        z_ref[t, q * 64 : (q + 1) * 64, :] = v[:64, :128] + (v[:64, 128:] + v[64:, :128])


def column_bands(table_ref, z_ref, low_ref, r, c):
    for t in range(8):
        y = times_table(z_ref[t], table_ref[COLS, :])
        for q in range(4):
            low_ref[t, q * 16 : (q + 1) * 16, :] = pick_lanes(
                [y[q * 64 + kk * 16 : q * 64 + (kk + 1) * 16] for kk in range(4)]
            )
        low_ref[t] = low_ref[t] * band_mask(r[4 * t : 4 * t + 4], c[4 * t : 4 * t + 4])


def moment_band_kernel(m_hbm, a_hbm, anchor_ref, table_ref, low_ref, act_ref, *scratch):
    m_ref, a_ref, z_ref, sems = scratch
    get_m = [
        pltpu.make_async_copy(m_hbm.at[pl.ds(t * 1024, 1024)], m_ref.at[t], sems.at[t])
        for t in range(8)
    ]
    get_a = pltpu.make_async_copy(a_hbm, a_ref, sems.at[8])
    get_a.start()
    for copy in get_m:
        copy.start()
    r, c = anchor_lanes(anchor_ref)
    get_a.wait()
    for q in range(4):
        v = lax.dot_general(
            table_ref[ROWS, :], a_ref[:, q * 256 : (q + 1) * 256], NT, preferred_element_type=F32
        )
        rows = slice(q * 64, (q + 1) * 64)
        act_ref[0, rows, :], act_ref[1, rows, :] = split(v[:64] + v[64:])
    for t in range(8):
        get_m[t].wait()
        row_bands(m_ref.at[t], table_ref, z_ref, t)
    column_bands(table_ref, z_ref, low_ref, r, c)
    low_ref[...] = DECAY * low_ref[...]


def send_kernel(cot_hbm, w_hbm, o_hbm, cot_ref, w_ref, sems):
    part = w_ref.shape[1]
    at = pl.multiple_of(share_index(part) * part, part)
    get_w = pltpu.make_async_copy(w_hbm.at[:, pl.ds(at, part)], w_ref, sems.at[0])
    get_cot = pltpu.make_async_copy(cot_hbm, cot_ref, sems.at[1])
    put_w = pltpu.make_async_copy(w_ref, o_hbm.at[:, pl.ds(512, part)], sems.at[2])
    put_cot = [
        pltpu.make_async_copy(cot_ref, o_hbm.at[j, pl.ds(0, 512)], sems.at[3 + j])
        for j in range(8)
    ]
    get_cot.start()
    get_w.start()
    get_cot.wait()
    for copy in put_cot:
        copy.start()
    get_w.wait()
    put_w.start()
    for copy in put_cot:
        copy.wait()
    put_w.wait()


def share_index(part, core=0, z=0):
    pairs = 1024 // (part * lax.axis_size("c"))
    mine = jnp.bitwise_xor(lax.axis_index("c"), core) * pairs
    if pairs > 1:
        mine = mine + jnp.bitwise_xor(lax.rem(lax.axis_index("z"), 2), z)
    return mine


def grad_band_kernel(act_ref, cot_ref, table_ref, out):
    high, low = act_ref[0], act_ref[1]
    for j in range(0, 8, 2):
        halves = []
        for i in range(2):
            both = mm(cot_ref[j + i, :512, :], table_ref[...])
            halves.append(split(both[:, :128] + both[:, 128:]))
        rh = jnp.concatenate([halves[0][0], halves[1][0]], axis=1)
        rl = jnp.concatenate([halves[0][1], halves[1][1]], axis=1)
        x = mm(high, rh) + (mm(high, rl) + mm(low, rh))
        for i in range(2):
            for q in range(4):
                out[j + i, q * 16 : (q + 1) * 16, :] = pick_lanes(
                    [
                        x[q * 64 + kk * 16 : q * 64 + (kk + 1) * 16, i * 128 : (i + 1) * 128]
                        for kk in range(4)
                    ]
                )


def pack_kernel(moment_hbm, grad_ref, anchor_ref, low_ref, keep_ref, give_ref, *scratch):
    moment_ref, pack_ref, sem = scratch
    get = pltpu.make_async_copy(moment_hbm, moment_ref, sem)
    get.start()
    r, c = anchor_lanes(anchor_ref)
    get.wait()
    for t in range(8):
        mask = band_mask(r[4 * t : 4 * t + 4], c[4 * t : 4 * t + 4])
        low_ref[t] = mask * grad_ref[t] + moment_ref[t]
    rows = low_ref[...].reshape(8, 4, 2, 8, 128)
    rows = (rows[:, :, 0] + rows[:, :, 1]).reshape(2, 128, 128)
    a, b = rows[0], rows[1]
    lane = lax.broadcasted_iota(jnp.int32, a.shape, 1)
    pack_ref[...] = jnp.where(lane % 16 < 8, a + pltpu.roll(a, 120, 1), b + pltpu.roll(b, 8, 1))
    core = lax.axis_index("c")
    keep_ref[...] = pack_ref[core_rows(core), :]
    give_ref[...] = pack_ref[core_rows(1 - core), :]


def core_rows(core):
    return pl.ds(pl.multiple_of(core * 64, 64), 64)


def unpack(p):
    low = lax.broadcasted_iota(jnp.int32, p.shape, 1) % 16 < 8
    a = jnp.where(low, p, pltpu.roll(p, 8, 1))
    b = jnp.where(low, pltpu.roll(p, 120, 1), p)
    r = jnp.concatenate([a, b], axis=0).reshape(8, 4, 1, 8, 128)
    return jnp.broadcast_to(r, (8, 4, 2, 8, 128)).reshape(8, 64, 128)


def rebuild(low_ref, table_ref, v_ref, emit):
    for t in range(8):
        spread = []
        for q in range(4):
            part = low_ref[t, q * 16 : (q + 1) * 16, :]
            spread += [jnp.where(lane_block(part.shape, kk), part, 0.0) for kk in range(4)]
        v = times_table(jnp.concatenate(spread, axis=0), table_ref[COLS_T, :])
        for n in range(2):
            rows = [v[(2 * n + i) * 64 : (2 * n + i + 1) * 64] for i in range(2)]
            hi, lo = split(jnp.concatenate(rows, axis=1))
            v_ref[t, n] = jnp.concatenate([hi, hi, lo], axis=0)
    for t in range(8):
        for n in range(2):
            both = mm(table_ref[ROWS_T, :192], v_ref[t, n])
            emit(t, 2 * n, both[:, :128])
            emit(t, 2 * n + 1, both[:, 128:])


def rest_kernel(low_ref, m_hbm, table_hbm, o_hbm, table_ref, m_ref, v_ref, sems):
    get_table = pltpu.make_async_copy(table_hbm, table_ref, sems.at[1])
    get_m = [
        pltpu.make_async_copy(m_hbm.at[pl.ds(t * 1024, 1024)], m_ref.at[t], sems.at[2 + t])
        for t in range(8)
    ]
    put = [pltpu.make_async_copy(m_ref.at[t], o_hbm.at[t], sems.at[10 + t]) for t in range(8)]
    for copy in [get_table] + get_m:
        copy.start()
    get_table.wait()

    def emit(t, q, v):
        if q == 0:
            get_m[t].wait()
        rows = slice(q * 256, (q + 1) * 256)
        m_ref[t, rows, :] = DECAY * m_ref[t, rows, :] - v
        if q == 3:
            put[t].start()

    rebuild(low_ref, table_ref, v_ref, emit)
    for copy in put:
        copy.wait()


def step_kernel(mine_ref, other_ref, anchor_ref, table_hbm, o_hbm, *scratch):
    low_ref, pack_ref, table_ref, v_ref, o_ref, sems = scratch
    get_table = pltpu.make_async_copy(table_hbm, table_ref, sems.at[8])
    put = [
        pltpu.make_async_copy(o_ref.at[t], o_hbm.at[pl.ds(t * 1024, 1024)], sems.at[t])
        for t in range(8)
    ]
    get_table.start()
    core = lax.axis_index("c")
    pack_ref[core_rows(core), :] = mine_ref[...]
    pack_ref[core_rows(1 - core), :] = other_ref[...]
    r, c = anchor_lanes(anchor_ref)
    low_ref[...] = unpack(pack_ref[...])
    for t in range(8):
        low_ref[t] = low_ref[t] * band_mask(r[4 * t : 4 * t + 4], c[4 * t : 4 * t + 4])
    get_table.wait()

    def emit(t, q, v):
        o_ref[t, q * 256 : (q + 1) * 256, :] = v.astype(BF16)
        if q == 3:
            put[t].start()

    rebuild(low_ref, table_ref, v_ref, emit)
    for copy in put:
        copy.wait()


def input_kernel(cot_hbm, *refs):
    count = len(refs) - 5
    w_hbm, o_hbm = refs[:count], refs[count]
    cot_ref, w_ref, o_ref, sems = refs[count + 1 :]
    part = w_ref.shape[2]
    get_cot = [
        pltpu.make_async_copy(
            cot_hbm.at[j, pl.ds(0, 512)], cot_ref.at[:, pl.ds(j * 128, 128)], sems.at[j]
        )
        for j in range(8)
    ]
    get_w = [pltpu.make_async_copy(w_hbm[n], w_ref.at[n], sems.at[8 + n]) for n in range(count)]
    for copy in get_cot + get_w:
        copy.start()
    put = []
    for copy in get_cot:
        copy.wait()
    for n in range(count):
        get_w[n].wait()
        rhs = jnp.concatenate([w_ref[n, j] for j in range(8)], axis=1)
        v = lax.dot_general(cot_ref[...], rhs, NT, preferred_element_type=F32)
        o_ref[n] = v.astype(BF16)
        share = share_index(part, n % 2, n // 2)
        lanes = pl.ds(pl.multiple_of(share * part, part), part)
        put.append(pltpu.make_async_copy(o_ref.at[n], o_hbm.at[:, lanes], sems.at[12 + n]))
        put[-1].start()
    for copy in put:
        copy.wait()


HBM = pl.BlockSpec(memory_space=pltpu.HBM)
VMEM = pl.BlockSpec(memory_space=pltpu.VMEM)


def whole(a):
    return pl.BlockSpec(a.shape, lambda i: (0,) * a.ndim)


def params(mib=16):
    return pltpu.CompilerParams(vmem_limit_bytes=mib * 2**20)


def cost(mflops, kib):
    return pl.CostEstimate(
        flops=mflops * 10**6, bytes_accessed=kib * 2**10, transcendentals=0
    )


def exchange_sum(v, axes, sizes, move):
    n = int(np.prod([sizes[a] for a in axes]))
    if move >= n:
        return v
    return v + lax.ppermute(v, axes, [(i, i ^ move) for i in range(n)])


def body(sizes, activations, cotangent, weight, momentum, band_anchor):
    table = jnp.asarray(tables())
    nz, nc = sizes["z"], sizes["c"]
    moment0 = momentum[0]
    anchor = band_anchor.transpose(1, 2, 0)

    pairs = 2 if nz > 1 else 1
    part = 1024 // (pairs * nc)
    with jax.named_scope("gather_cotangent"):
        sent = pl.pallas_call(
            send_kernel,
            in_specs=[HBM] * 2,
            out_specs=HBM,
            out_shape=jax.ShapeDtypeStruct((8, 512 + part, 128), BF16),
            scratch_shapes=[
                pltpu.VMEM((512, 128), BF16),
                pltpu.VMEM((8, part, 128), BF16),
                pltpu.SemaphoreType.DMA((11,)),
            ],
            compiler_params=params(56),
            cost_estimate=cost(1, 2048),
        )(cotangent, weight.reshape(8, 1024, 128))
        got = lax.all_to_all(sent, TENSOR, 0, 0)

    with jax.named_scope("moment_band"):
        moment_band, act_band = pl.pallas_call(
            moment_band_kernel,
            in_specs=[HBM, HBM, VMEM, VMEM],
            out_specs=[VMEM] * 2,
            out_shape=[
                jax.ShapeDtypeStruct((8, 64, 128), F32),
                jax.ShapeDtypeStruct((2, 256, 512), BF16),
            ],
            scratch_shapes=[
                pltpu.VMEM((8, 1024, 128), F32),
                pltpu.VMEM((512, 1024), BF16),
                pltpu.VMEM((8, 256, 128), F32),
                pltpu.SemaphoreType.DMA((9,)),
            ],
            compiler_params=params(52),
            cost_estimate=cost(2000, 5120),
        )(moment0, activations, anchor, table)
        got, moment_band, act_band = lax.optimization_barrier((got, moment_band, act_band))

    own_scale = jnp.maximum(jnp.max(jnp.abs(cotangent), axis=0).astype(F32), 1e-30) / LIMIT

    swap = [(i, nc - 1 - i) for i in range(nc)]
    with jax.named_scope("weight_share"):
        share = got[:, 512:]
        shares = [share, lax.ppermute(share, "c", swap)]
        if pairs > 1:
            share = lax.ppermute(share, "z", [(k, k ^ 1) for k in range(nz)])
            shares += [share, lax.ppermute(share, "c", swap)]

    with jax.named_scope("grad_band"):
        grad_band = pl.pallas_call(
            grad_band_kernel,
            out_shape=jax.ShapeDtypeStruct((8, 64, 128), F32),
            compiler_params=params(24),
            cost_estimate=cost(2000, 2048),
        )(act_band, got, jnp.asarray(tables()[COLS]))
        got, grad_band = lax.optimization_barrier((got, grad_band))
        grad_band = lax.all_to_all(grad_band, TENSOR, 0, 0)

    with jax.named_scope("weight_grad"):
        cot8 = got[:, :512]
        top = jnp.max(jnp.abs(cot8), axis=1).astype(F32)
        top = jnp.maximum(top, 1e-30)
        grad = jnp.einsum("tf,jtc->fjc", activations, cot8, preferred_element_type=F32)
        grad = jnp.moveaxis((grad * (LIMIT / top)).astype(F16), 1, 0)
        grad, grad_band, shares = lax.optimization_barrier((grad, grad_band, shares))
        grad = lax.all_to_all(grad, TENSOR, 0, 0)

    with jax.named_scope("pack"):
        low, mine, other = pl.pallas_call(
            pack_kernel,
            in_specs=[HBM, VMEM, VMEM],
            out_specs=[VMEM] * 3,
            out_shape=[jax.ShapeDtypeStruct((8, 64, 128), F32)]
            + [jax.ShapeDtypeStruct((64, 128), F32)] * 2,
            scratch_shapes=[
                pltpu.VMEM((8, 64, 128), F32),
                pltpu.VMEM((128, 128), F32),
                pltpu.SemaphoreType.DMA,
            ],
            compiler_params=params(),
            cost_estimate=cost(100, 1024),
        )(moment_band, grad_band, anchor)

    with jax.named_scope("rest"):
        rest = pl.pallas_call(
            rest_kernel,
            in_specs=[VMEM, HBM, HBM],
            out_specs=HBM,
            out_shape=jax.ShapeDtypeStruct((8, 1024, 128), F32),
            scratch_shapes=[
                pltpu.VMEM(table.shape, BF16),
                pltpu.VMEM((8, 1024, 128), F32),
                pltpu.VMEM((8, 2, 192, 256), BF16),
                pltpu.SemaphoreType.DMA((18,)),
            ],
            compiler_params=params(52),
            cost_estimate=cost(3000, 8192),
        )(low, moment0, table)

    with jax.named_scope("input_grad"):
        input_grad = pl.pallas_call(
            input_kernel,
            in_specs=[HBM] * (1 + len(shares)),
            out_specs=HBM,
            out_shape=jax.ShapeDtypeStruct((512, 1024), BF16),
            scratch_shapes=[
                pltpu.VMEM((512, 1024), BF16),
                pltpu.VMEM((len(shares), 8, part, 128), BF16),
                pltpu.VMEM((len(shares), 512, part), BF16),
                pltpu.SemaphoreType.DMA((16,)),
            ],
            compiler_params=params(16),
            cost_estimate=cost(1000, 4096),
        )(got, *shares)

    with jax.named_scope("band_total"):
        mine = mine + lax.ppermute(other, "c", swap)
        mine = exchange_sum(mine, ("z",), sizes, 1)
        mine, rest = lax.optimization_barrier((mine, rest))
        mine = exchange_sum(mine, ("z",), sizes, 3)
        mine, input_grad = lax.optimization_barrier((mine, input_grad))
        mine = exchange_sum(mine, ("z",), sizes, 7)
        mine = exchange_sum(mine, ("yh",), sizes, 1)

    with jax.named_scope("new_momentum"):
        other = lax.ppermute(mine, "c", swap)
        new_momentum = rest + grad.astype(F32) * own_scale

    with jax.named_scope("weight_step"):
        weight_step = pl.pallas_call(
            step_kernel,
            in_specs=[VMEM] * 3 + [HBM],
            out_specs=HBM,
            out_shape=jax.ShapeDtypeStruct((8192, 128), BF16),
            scratch_shapes=[
                pltpu.VMEM((8, 64, 128), F32),
                pltpu.VMEM((128, 128), F32),
                pltpu.VMEM(table.shape, BF16),
                pltpu.VMEM((8, 2, 192, 256), BF16),
                pltpu.VMEM((8, 1024, 128), BF16),
                pltpu.SemaphoreType.DMA((10,)),
            ],
            compiler_params=params(16),
            cost_estimate=cost(3000, 2048),
        )(mine, other, anchor, table)

    return (input_grad, new_momentum.reshape(1, 8192, 128), weight_step)


def solution(mesh):
    shape = (2, 8, 2, 4, 2)
    if mesh.devices.size == 16:
        shape = (1, 1, 2, 4, 2)
    names = ("yh", "z", "c", "x", "yl")
    fine = Mesh(mesh.devices.reshape(shape), names)
    dp = ("yh", "z", "c")
    return jax.shard_map(
        functools.partial(body, dict(zip(names, shape))),
        mesh=fine,
        in_specs=(
            P(dp, TENSOR),
            P(dp, TENSOR),
            P(None, TENSOR),
            P(dp, None, TENSOR),
            P(None, TENSOR, None),
        ),
        out_specs=(P(dp, TENSOR), P(dp, None, TENSOR), P(None, TENSOR)),
        check_vma=False,
    )
```
